512 devices in a mesh: dp: 8 (over z), expert: 64 (over x, y, core).
Axes of the slice: x: 4, y: 8, z: 8, core: 2. Of those that a mesh axis runs over, the one named last changes fastest.
Arguments:
- tokens: bfloat16 [2048, 2048], P('expert', 'dp'), may hold values from -6 to 6
- cotangent: bfloat16 [2048, 2048], P('expert', 'dp'), may hold values from -6 to 6
- routes: int32 [2048, 8], P('expert'), may hold values from 0 to 63, all different within a row; in each aligned block of 32 rows (0 to 31, 32 to 63, ...) at most 5 rows name the same one
- probs: float32 [2048, 8], P('expert'), may hold values from 0.03 to 0.6
- matching: int32 [64], replicated, may hold values from 0 to 63, as said below
- gate_weight: bfloat16 [64, 2048, 1024], P('expert', None, 'dp'), may hold values from -0.125 to 0.125
- up_weight: bfloat16 [64, 2048, 1024], P('expert', None, 'dp'), may hold values from -0.125 to 0.125
- down_weight: bfloat16 [64, 2048, 1024], P('expert', None, 'dp'), may hold values from -0.1875 to 0.1875
Outputs:
- input_grad: bfloat16 [2048, 2048], P('expert', 'dp')
- gate_weight_grad: float32 [64, 2048, 1024], P('expert', None, 'dp')
- up_weight_grad: float32 [64, 2048, 1024], P('expert', None, 'dp')
- down_weight_grad: float32 [64, 2048, 1024], P('expert', None, 'dp')
The draws below stay inside these ranges and needn't reach their ends.
Inputs may be any that keep to these rules, and one draw needn't show every extreme that they name: matching pairs the experts: matching[matching[i]] == i and matching[i] != i. `routes`: each token names 8 different experts; within each aligned block of 32 tokens no expert is named by more than 5 tokens.
All inputs are finite; a program needn't handle non-finite values.
Results may differ from the reference program's by a relative error of at most 0.015.
Values may be sent and summed in bfloat16 or wider, within the bound.
No kernel may reach another device: no remote copies, remote signals or barrier semaphores. Data moves between devices by JAX's collectives and lax.ppermute only.
A program may use at most 64 MiB of HBM per device.

```python
import math
import jax
import jax.numpy as jnp
import numpy as np
from jax import lax

D = 2048
HID = 1024
TOPK = 8
TOK_DEV = 32
EXPERTS = 64
CAP = 5
TOKENS = 2048
N_DP = 8
N_EXPERT = 64


def draw_matching(key, part):
    order = jax.random.permutation(key, EXPERTS).astype(jnp.int32)
    first = order[0::2]
    second = order[1::2]
    paired = jnp.zeros((EXPERTS,), jnp.int32).at[first].set(second).at[second].set(first)
    return paired.astype(jnp.int32)


def block_scale(stream_key, dims, cuts, low, top_value):
    gain, own = 1.0, jax.random.fold_in(stream_key, 6)
    for position, shards_of in cuts:
        draws = jnp.exp(jax.random.uniform(jax.random.fold_in(own, position), (shards_of,), jnp.float32, low / len(cuts), top_value / len(cuts)))
        gain = gain * jnp.repeat(draws, dims[position] // shards_of).reshape([-1 if axis == position else 1 for axis in range(len(dims))])
    return gain


def assign_block(own_key, own, number, rows, amount, top, most, slope):
    ranking = jax.random.permutation(own_key, amount)
    heavy_load, common = load_shares(amount, rows * top, most, slope, True), load_shares(amount, rows * top, most, slope, False)
    places = jnp.arange(amount)

    def named(sizes, turn):
        used = int((sizes > 0).sum())
        fixed = max(1, used // 4)
        passed = fixed + (places - fixed + turn * (used - fixed)) % max(1, amount - fixed)
        return jnp.zeros((amount,), jnp.int32).at[ranking[jnp.where(places < fixed, places, passed)]].set(jnp.asarray(sizes, jnp.int32))

    sizes = jnp.where(number % 4 == 0, named(heavy_load, number // 4), named(common, number - number // 4 - 1))
    mixed = jax.random.permutation(jax.random.fold_in(own, 3), amount)
    source_of, taker = mixed[0:amount // 2 * 2:2], mixed[1:amount // 2 * 2:2]
    margin = jnp.minimum(sizes[source_of] - 1, most - sizes[taker]) // 2
    margin = jnp.where((source_of == ranking[0]) | (taker == ranking[0]) | (sizes[taker] == 0), 0, jnp.maximum(margin, 0))
    passed = jax.random.randint(jax.random.fold_in(own, 4), (amount // 2,), 0, 1 << 20) % (margin + 1)
    sizes = sizes.at[source_of].add(-passed).at[taker].add(passed)
    labels = jnp.searchsorted(jnp.cumsum(sizes), jnp.arange(rows * top), side="right").astype(jnp.int32)
    grid = labels.reshape(top, rows).T
    grid = grid[jax.random.permutation(jax.random.fold_in(own, 1), rows)]
    turn = jax.random.randint(jax.random.fold_in(own, 2), (rows, 1), 0, top)
    return jnp.take_along_axis(grid, (jnp.arange(top)[None, :] + turn) % top, axis=1)


def load_shares(count, total, most, skew, full):
    portions = [(1 << 20) // math.isqrt(grade ** skew) + 1 for grade in range(1, count + 1)]
    largest = most if full else min(most, max(-(-total // count), total * portions[0] // sum(portions)))
    least = 1 if total - largest >= count - 1 else 0
    holding, spare = [largest] + [least] * (count - 1), total - largest - least * (count - 1)
    while spare > 0:
        free = [i for i in range(1, count) if holding[i] < largest] or [i for i in range(1, count) if holding[i] < most]
        pool, left = sum([portions[i] for i in free]), spare
        for i in free:
            addition = min(most - holding[i], max(1, left * portions[i] // pool), spare)
            holding[i] = holding[i] + addition
            spare = spare - addition
    return np.array(holding)


def normal_values(key, extent, deviation, bound, split=(), kind=jnp.bfloat16):
    drawn = deviation * jax.random.normal(key, extent, jnp.float32)
    if split:
        drawn = drawn * block_scale(key, extent, split, -0.22, 0.18)
    return jnp.clip(drawn, -bound, bound).astype(kind)


def setup_inputs(seed: int = 0) -> dict:
    arg_keys = jax.random.split(jax.random.key(seed), 9)
    tokens = normal_values(arg_keys[0], (TOKENS, D), 1.0, 6.0, ((0, 64), (1, 8)))
    cotangent = normal_values(arg_keys[1], (TOKENS, D), 1.0, 6.0, ((0, 64), (1, 8)))
    routes_keys = jax.random.split(jax.random.fold_in(arg_keys[2], 1), TOKENS // TOK_DEV)
    routes_turns = jax.random.permutation(jax.random.fold_in(arg_keys[2], 3), TOKENS // TOK_DEV)
    routes = jax.vmap(lambda own, number: assign_block(jax.random.fold_in(arg_keys[2], 2), own, number, TOK_DEV, EXPERTS, TOPK, CAP, 2))(routes_keys, routes_turns).reshape((TOKENS, TOPK))
    probs = jnp.clip(jnp.exp(math.log(0.6) - 2.9957323 * jax.random.uniform(arg_keys[3], (TOKENS, TOPK), jnp.float32) ** block_scale(arg_keys[3], (TOKENS, TOPK), ((0, 64),), -0.2, 0.2)), 0.03, 0.6)
    matching = draw_matching(jax.random.fold_in(arg_keys[8], 71), 0)
    gate_weight = normal_values(arg_keys[5], (EXPERTS, D, HID), D ** -0.5, 0.125, ((0, 64), (2, 8)))
    up_weight = normal_values(arg_keys[6], (EXPERTS, D, HID), D ** -0.5, 0.125, ((0, 64), (2, 8)))
    down_weight = normal_values(arg_keys[7], (EXPERTS, D, HID), HID ** -0.5, 0.1875, ((0, 64), (2, 8)))
    return dict(tokens=tokens, cotangent=cotangent, routes=routes, probs=probs, matching=matching, gate_weight=gate_weight, up_weight=up_weight, down_weight=down_weight)


def reference(tokens, cotangent, routes, probs, matching, gate_weight, up_weight, down_weight):
    pair_total = TOKENS * TOPK
    width = N_EXPERT * CAP
    pair_expert = routes.reshape(pair_total).astype(jnp.int32)
    onehot = (pair_expert[:, None] == jnp.arange(EXPERTS, dtype=jnp.int32)[None, :]).astype(jnp.int32)
    running = jnp.cumsum(onehot.reshape(N_EXPERT, TOK_DEV * TOPK, EXPERTS), axis=1).reshape(pair_total, EXPERTS)
    rank = jnp.sum(onehot * running, axis=1) - 1
    source = jnp.arange(pair_total, dtype=jnp.int32) // (TOK_DEV * TOPK)
    slot = (pair_expert * width + source * CAP + rank).astype(jnp.int32)
    index = jnp.full((EXPERTS * width,), pair_total, jnp.int32).at[slot].set(jnp.arange(pair_total, dtype=jnp.int32))
    index = index.reshape(EXPERTS, width)
    pair_in = jnp.concatenate([jnp.repeat(tokens, TOPK, axis=0), jnp.zeros((1, D), jnp.bfloat16)], axis=0)
    scaled = jnp.repeat(cotangent.astype(jnp.float32), TOPK, axis=0) * probs.reshape(pair_total, 1)
    pair_out = jnp.concatenate([scaled.astype(jnp.bfloat16), jnp.zeros((1, D), jnp.bfloat16)], axis=0)
    slice_width = HID // N_DP
    contract_rows = (((0,), (0,)), ((), ()))

    def one_expert(carry, stuff):
        rows, w_gate, w_up, w_down = stuff
        inputs = pair_in[rows]
        grads = pair_out[rows]
        gate = jnp.dot(inputs, w_gate, preferred_element_type=jnp.float32)
        upper = jnp.dot(inputs, w_up, preferred_element_type=jnp.float32)
        sig = jax.nn.sigmoid(gate)
        hidden = (gate * sig * upper).astype(jnp.bfloat16)
        hidden_back = jnp.dot(grads, w_down, preferred_element_type=jnp.float32)
        up_back = (hidden_back * gate * sig).astype(jnp.bfloat16)
        gate_back = (hidden_back * upper * sig * (1.0 + gate * (1.0 - sig))).astype(jnp.bfloat16)
        gate_sum = lax.dot_general(inputs, gate_back, contract_rows, preferred_element_type=jnp.float32)
        up_sum = lax.dot_general(inputs, up_back, contract_rows, preferred_element_type=jnp.float32)
        down_sum = lax.dot_general(grads, hidden, contract_rows, preferred_element_type=jnp.float32)
        gate_slices = gate_back.astype(jnp.float32).reshape(width, N_DP, slice_width)
        up_slices = up_back.astype(jnp.float32).reshape(width, N_DP, slice_width)
        wg_slices = w_gate.astype(jnp.float32).reshape(D, N_DP, slice_width)
        wu_slices = w_up.astype(jnp.float32).reshape(D, N_DP, slice_width)
        slice_part = jnp.einsum("rsh,dsh->rsd", gate_slices, wg_slices) + jnp.einsum("rsh,dsh->rsd", up_slices, wu_slices)
        pair_back = jnp.sum(slice_part.astype(jnp.bfloat16).astype(jnp.float32), axis=1)
        carry = carry.at[rows].add(pair_back)
        return carry, (gate_sum, up_sum, down_sum)

    start = jnp.zeros((pair_total + 1, D), jnp.float32)
    carry, sums = lax.scan(one_expert, start, (index, gate_weight, up_weight, down_weight))
    input_grad = jnp.sum(carry[:pair_total].reshape(TOKENS, TOPK, D), axis=1).astype(jnp.bfloat16)
    gate_sums, up_sums, down_sums = sums
    return (input_grad, jnp.take(gate_sums, matching, axis=0), jnp.take(up_sums, matching, axis=0), jnp.take(down_sums, matching, axis=0))
```

```python
import jax
import jax.numpy as jnp
from jax import lax
from jax.experimental import pallas as pl
from jax.experimental.pallas import tpu as pltpu
from jax.sharding import PartitionSpec as P

BF = jnp.bfloat16
F32 = jnp.float32
CAP = 5
MIB = 1024 * 1024

contract_rows = (((0,), (0,)), ((), ()))
contract_cols = (((1,), (1,)), ((), ()))


def params():
    return pltpu.CompilerParams(vmem_limit_bytes=40 * MIB)


def vmem(n):
    return [pl.BlockSpec(memory_space=pltpu.VMEM)] * n


def dot(a, b, dims=(((1,), (0,)), ((), ()))):
    return lax.dot_general(a, b, dims, preferred_element_type=F32)


def pack_kernel(tok_ref, cot_ref, routes_ref, probs_ref, match_ref, send_ref, pick_ref):
    dests = match_ref.shape[1]
    rows = tok_ref.shape[0]
    width = tok_ref.shape[1]
    eye = lax.broadcasted_iota(jnp.int32, (dests, dests), 0) == lax.broadcasted_iota(
        jnp.int32, (dests, dests), 1
    )
    wanted = jnp.sum(jnp.where(eye, match_ref[...], 0), axis=1, keepdims=True)
    named = jnp.zeros((dests, rows), F32)
    weight = jnp.zeros((dests, rows), F32)
    for k in range(routes_ref.shape[0]):
        hit = wanted == routes_ref[k : k + 1, :]
        named = named + jnp.where(hit, 1.0, 0.0)
        weight = weight + jnp.where(hit, probs_ref[k : k + 1, :], 0.0)
    before = lax.broadcasted_iota(jnp.int32, (rows, rows), 0) < lax.broadcasted_iota(
        jnp.int32, (rows, rows), 1
    )
    rank = dot(named.astype(BF), jnp.where(before, 1.0, 0.0).astype(BF))
    for c in range(CAP):
        pick = jnp.where((named > 0.5) & (jnp.abs(rank - c) < 0.5), 1.0, 0.0)
        scale = jnp.sum(pick * weight, axis=1, keepdims=True)
        pick = pick.astype(BF)
        pick_ref[c * dests : (c + 1) * dests, :] = pick
        send_ref[:, c * width : (c + 1) * width] = dot(pick, tok_ref[...]).astype(BF)
        grads = dot(pick, cot_ref[...]) * scale
        send_ref[:, (CAP + c) * width : (CAP + c + 1) * width] = grads.astype(BF)


def pack(tokens, cotangent, routes, probs, matching):
    dests = matching.shape[0]
    rows, width = tokens.shape
    return pl.pallas_call(
        pack_kernel,
        out_shape=(
            jax.ShapeDtypeStruct((dests, 2 * CAP * width), BF),
            jax.ShapeDtypeStruct((CAP * dests, rows), BF),
        ),
        in_specs=vmem(5),
        out_specs=tuple(vmem(2)),
        compiler_params=params(),
    )(tokens, cotangent, routes.T, probs.T, matching.reshape(1, dests))


def reorder_kernel(match_ref, src_ref, dst_ref, sems):
    count, rows = dst_ref.shape[0], dst_ref.shape[1]
    copies = [
        pltpu.make_async_copy(
            src_ref.at[match_ref[d], pl.ds(0, rows)], dst_ref.at[d], sems.at[d]
        )
        for d in range(count)
    ]
    for c in copies:
        c.start()
    for c in copies:
        c.wait()


def reorder(arrived, matching, rows):
    count, _, lanes = arrived.shape
    return pl.pallas_call(
        reorder_kernel,
        out_shape=jax.ShapeDtypeStruct((count, rows, lanes), BF),
        in_specs=[
            pl.BlockSpec(memory_space=pltpu.SMEM),
            pl.BlockSpec(memory_space=pl.ANY),
        ],
        out_specs=pl.BlockSpec(memory_space=pl.ANY),
        scratch_shapes=[pltpu.SemaphoreType.DMA((count,))],
        compiler_params=params(),
        cost_estimate=pl.CostEstimate(
            flops=0, bytes_accessed=4 * count * rows * lanes, transcendentals=0
        ),
    )(matching, arrived)


def stack_slots(block, first, width):
    return jnp.concatenate(
        [block[:, (first + c) * width : (first + c + 1) * width] for c in range(CAP)], axis=0
    )


def expert_kernel(rows_ref, w_ref, back_ref, pair_ref, hidden_ref):
    slices, sources, _ = rows_ref.shape
    width = rows_ref.shape[2] // (2 * CAP)
    per = w_ref.shape[0] // slices
    part = w_ref.shape[1] // 3
    lanes = w_ref.shape[2]

    def weight(z, which):
        return w_ref[z * per : (z + 1) * per, which * part : (which + 1) * part, :].reshape(
            per * part, lanes
        )

    def both(z):
        return jnp.concatenate([weight(z, 0), weight(z, 1)], axis=1)

    two = jnp.zeros((CAP * sources, 2 * lanes), F32)
    hidden_back = jnp.zeros((CAP * sources, lanes), F32)
    for z in range(slices):
        block = rows_ref[z]
        two = two + dot(stack_slots(block, 0, width), both(z))
        hidden_back = hidden_back + dot(stack_slots(block, CAP, width), weight(z, 2))
    gate, upper = two[:, :lanes], two[:, lanes:]
    sig = jax.nn.sigmoid(gate)
    hidden_ref[...] = (gate * sig * upper).astype(BF)
    up_back = (hidden_back * gate * sig).astype(BF)
    gate_back = (hidden_back * upper * sig * (1.0 + gate * (1.0 - sig))).astype(BF)
    pair = jnp.concatenate([gate_back, up_back], axis=1)
    pair_ref[...] = pair
    for z in range(slices):
        parts = dot(pair, both(z), contract_cols).astype(BF)
        for c in range(CAP):
            back_ref[z, :, c * width : (c + 1) * width] = parts[c * sources : (c + 1) * sources, :]


def expert(rows, weights):
    slices, sources, lanes = rows.shape
    hidden = weights.shape[2]
    return pl.pallas_call(
        expert_kernel,
        out_shape=(
            jax.ShapeDtypeStruct((slices, sources, lanes // 2), BF),
            jax.ShapeDtypeStruct((CAP * sources, 2 * hidden), BF),
            jax.ShapeDtypeStruct((CAP * sources, hidden), BF),
        ),
        in_specs=vmem(2),
        out_specs=tuple(vmem(3)),
        compiler_params=params(),
    )(rows, weights)


def outer_kernel(rows_ref, pair_ref, hidden_ref, gate_ref, up_ref, down_ref):
    width = rows_ref.shape[2] // (2 * CAP)
    lanes = hidden_ref.shape[1]
    block = rows_ref[0]
    two = dot(stack_slots(block, 0, width), pair_ref[...], contract_rows)
    gate_ref[0] = two[:, :lanes]
    up_ref[0] = two[:, lanes:]
    down_ref[0] = dot(stack_slots(block, CAP, width), hidden_ref[...], contract_rows)


def outer(rows, pair, hidden):
    slices, sources, lanes = rows.shape
    width = lanes // (2 * CAP)
    units = hidden.shape[1]
    out = jax.ShapeDtypeStruct((1, slices * width, units), F32)
    flops = 2 * CAP * sources * slices * width * units * 3
    return pl.pallas_call(
        outer_kernel,
        grid=(slices,),
        out_shape=(out,) * 3,
        in_specs=[
            pl.BlockSpec((1, sources, lanes), lambda z: (z, 0, 0)),
            pl.BlockSpec(pair.shape, lambda z: (0, 0)),
            pl.BlockSpec(hidden.shape, lambda z: (0, 0)),
        ],
        out_specs=(pl.BlockSpec((1, width, units), lambda z: (0, z, 0)),) * 3,
        compiler_params=params(),
        cost_estimate=pl.CostEstimate(
            flops=flops, bytes_accessed=rows.size * 2 + 12 * slices * width * units, transcendentals=0
        ),
    )(rows, pair, hidden)


def combine_kernel(back_ref, pick_ref, out_ref):
    slices = back_ref.shape[0]
    width = out_ref.shape[1]
    pick = pick_ref[...]
    total = jnp.zeros(out_ref.shape, F32)
    for z in range(slices):
        total = total + dot(pick, stack_slots(back_ref[z], 0, width), contract_rows)
    out_ref[...] = total.astype(BF)


def combine(back, pick, shape):
    return pl.pallas_call(
        combine_kernel,
        out_shape=jax.ShapeDtypeStruct(shape, BF),
        in_specs=vmem(2),
        out_specs=pl.BlockSpec(memory_space=pltpu.VMEM),
        compiler_params=params(),
    )(back, pick)


def swap(x, axes):
    return lax.all_to_all(x, axes, split_axis=0, concat_axis=0, tiled=True)


def local(tokens, cotangent, routes, probs, matching, gate_weight, up_weight, down_weight):
    experts = matching.shape[0]
    model_width, units = gate_weight.shape[1:]
    slices = model_width // tokens.shape[1]
    piece = model_width // experts
    send, pick = pack(tokens, cotangent, routes, probs, matching)
    lanes = send.shape[1]
    first = jnp.concatenate(
        [w.reshape(experts, piece, units) for w in (gate_weight, up_weight, down_weight)]
        + [send.reshape(experts, lanes // units, units)],
        axis=1,
    )
    arrived = swap(first, "expert")
    rows = arrived[:, 3 * piece :, :].reshape(1, experts, lanes)
    rows = lax.all_gather(rows, "dp", axis=0, tiled=True)
    weights = swap(reorder(arrived, matching, 3 * piece), "expert")
    back, pair, hidden = expert(rows, weights)
    back = swap(back.reshape(slices * experts, 2, lanes // 4), ("dp", "expert"))
    gate_sum, up_sum, down_sum = outer(rows, pair, hidden)
    total = combine(back.reshape(slices, experts, lanes // 2), pick, tokens.shape)
    return (total, gate_sum, up_sum, down_sum)


def solution(mesh):
    placed = (
        P("expert", "dp"),
        P("expert", "dp"),
        P("expert", None),
        P("expert", None),
        P(),
        P("expert", None, "dp"),
        P("expert", None, "dp"),
        P("expert", None, "dp"),
    )
    return jax.shard_map(
        local,
        mesh=mesh,
        in_specs=placed,
        out_specs=(
            P("expert", "dp"),
            P("expert", None, "dp"),
            P("expert", None, "dp"),
            P("expert", None, "dp"),
        ),
        check_vma=False,
    )
```

```python
import jax
import jax.numpy as jnp
from jax import lax
from jax.experimental import pallas as pl
from jax.experimental.pallas import tpu as pltpu
from jax.sharding import PartitionSpec as P

BF = jnp.bfloat16
F32 = jnp.float32
CAP = 5
MIB = 1024 * 1024

contract_rows = (((0,), (0,)), ((), ()))
contract_cols = (((1,), (1,)), ((), ()))


def params():
    return pltpu.CompilerParams(vmem_limit_bytes=40 * MIB)


def vmem(n):
    return [pl.BlockSpec(memory_space=pltpu.VMEM)] * n


def dot(a, b, dims=(((1,), (0,)), ((), ()))):
    return lax.dot_general(a, b, dims, preferred_element_type=F32)


def pack_kernel(
    tok_hbm, cot_hbm, routes_hbm, probs_hbm, match_hbm,
    send_ref, pick_ref,
    tok_ref, cot_ref, routes_ref, probs_ref, match_ref, sems,
):
    pairs = (
        (routes_hbm, routes_ref),
        (probs_hbm, probs_ref),
        (match_hbm, match_ref),
        (tok_hbm, tok_ref),
        (cot_hbm, cot_ref),
    )
    copies = [pltpu.make_async_copy(a, b, sems.at[i]) for i, (a, b) in enumerate(pairs)]
    for c in copies:
        c.start()
    for c in copies:
        c.wait()
    dests = match_ref.shape[1]
    rows = tok_ref.shape[0]
    width = tok_ref.shape[1]
    eye = lax.broadcasted_iota(jnp.int32, (dests, dests), 0) == lax.broadcasted_iota(
        jnp.int32, (dests, dests), 1
    )
    wanted = jnp.sum(jnp.where(eye, match_ref[...], 0), axis=1, keepdims=True)
    named = jnp.zeros((dests, rows), F32)
    weight = jnp.zeros((dests, rows), F32)
    for k in range(routes_ref.shape[0]):
        hit = wanted == routes_ref[k : k + 1, :]
        named = named + jnp.where(hit, 1.0, 0.0)
        weight = weight + jnp.where(hit, probs_ref[k : k + 1, :], 0.0)
    before = lax.broadcasted_iota(jnp.int32, (rows, rows), 0) < lax.broadcasted_iota(
        jnp.int32, (rows, rows), 1
    )
    rank = dot(named.astype(BF), jnp.where(before, 1.0, 0.0).astype(BF))
    for c in range(CAP):
        pick = jnp.where((named > 0.5) & (jnp.abs(rank - c) < 0.5), 1.0, 0.0)
        scale = jnp.sum(pick * weight, axis=1, keepdims=True)
        pick = pick.astype(BF)
        pick_ref[c * dests : (c + 1) * dests, :] = pick
        send_ref[:, c * width : (c + 1) * width] = dot(pick, tok_ref[...]).astype(BF)
        grads = dot(pick, cot_ref[...]) * scale
        send_ref[:, (CAP + c) * width : (CAP + c + 1) * width] = grads.astype(BF)


def pack(tokens, cotangent, routes, probs, matching):
    dests = matching.shape[0]
    rows, width = tokens.shape
    return pl.pallas_call(
        pack_kernel,
        out_shape=(
            jax.ShapeDtypeStruct((dests, 2 * CAP * width), BF),
            jax.ShapeDtypeStruct((CAP * dests, rows), BF),
        ),
        in_specs=[pl.BlockSpec(memory_space=pltpu.HBM)] * 5,
        out_specs=tuple(vmem(2)),
        scratch_shapes=[
            pltpu.VMEM(tokens.shape, BF),
            pltpu.VMEM(tokens.shape, BF),
            pltpu.VMEM(routes.shape[::-1], jnp.int32),
            pltpu.VMEM(routes.shape[::-1], F32),
            pltpu.VMEM((1, dests), jnp.int32),
            pltpu.SemaphoreType.DMA((5,)),
        ],
        compiler_params=params(),
    )(tokens, cotangent, routes.T, probs.T, matching.reshape(1, dests))


def reorder_kernel(match_ref, src_ref, dst_ref, sems):
    count, rows = dst_ref.shape[0], dst_ref.shape[1]
    copies = [
        pltpu.make_async_copy(
            src_ref.at[match_ref[d], pl.ds(0, rows)], dst_ref.at[d], sems.at[d]
        )
        for d in range(count)
    ]
    for c in copies:
        c.start()
    for c in copies:
        c.wait()


def reorder(arrived, matching, rows):
    count, _, lanes = arrived.shape
    return pl.pallas_call(
        reorder_kernel,
        out_shape=jax.ShapeDtypeStruct((count, rows, lanes), BF),
        in_specs=[
            pl.BlockSpec(memory_space=pltpu.SMEM),
            pl.BlockSpec(memory_space=pl.ANY),
        ],
        out_specs=pl.BlockSpec(memory_space=pl.ANY),
        scratch_shapes=[pltpu.SemaphoreType.DMA((count,))],
        compiler_params=params(),
        cost_estimate=pl.CostEstimate(
            flops=0, bytes_accessed=4 * count * rows * lanes, transcendentals=0
        ),
    )(matching, arrived)


def stack_slots(block, first, width):
    return jnp.concatenate(
        [block[:, (first + c) * width : (first + c + 1) * width] for c in range(CAP)], axis=0
    )


def expert_kernel(rows_ref, w_ref, back_ref, pair_ref, hidden_ref):
    slices, sources, _ = rows_ref.shape
    width = rows_ref.shape[2] // (2 * CAP)
    per = w_ref.shape[0] // slices
    part = w_ref.shape[1] // 3
    lanes = w_ref.shape[2]

    def weight(z, which):
        return w_ref[z * per : (z + 1) * per, which * part : (which + 1) * part, :].reshape(
            per * part, lanes
        )

    def both(z):
        return jnp.concatenate([weight(z, 0), weight(z, 1)], axis=1)

    two = jnp.zeros((CAP * sources, 2 * lanes), F32)
    hidden_back = jnp.zeros((CAP * sources, lanes), F32)
    for z in range(slices):
        block = rows_ref[z]
        two = two + dot(stack_slots(block, 0, width), both(z))
        hidden_back = hidden_back + dot(stack_slots(block, CAP, width), weight(z, 2))
    gate, upper = two[:, :lanes], two[:, lanes:]
    sig = jax.nn.sigmoid(gate)
    hidden_ref[...] = (gate * sig * upper).astype(BF)
    up_back = (hidden_back * gate * sig).astype(BF)
    gate_back = (hidden_back * upper * sig * (1.0 + gate * (1.0 - sig))).astype(BF)
    pair = jnp.concatenate([gate_back, up_back], axis=1)
    pair_ref[...] = pair
    for z in range(slices):
        back_ref[z] = dot(pair, both(z), contract_cols).astype(BF)


def expert(rows, weights):
    slices, sources, lanes = rows.shape
    hidden = weights.shape[2]
    return pl.pallas_call(
        expert_kernel,
        out_shape=(
            jax.ShapeDtypeStruct((slices, CAP * sources, lanes // (2 * CAP)), BF),
            jax.ShapeDtypeStruct((CAP * sources, 2 * hidden), BF),
            jax.ShapeDtypeStruct((CAP * sources, hidden), BF),
        ),
        in_specs=vmem(2),
        out_specs=tuple(vmem(3)),
        compiler_params=params(),
    )(rows, weights)


def outer_kernel(rows_ref, pair_ref, hidden_ref, gate_ref, up_ref, down_ref):
    width = rows_ref.shape[2] // (2 * CAP)
    lanes = hidden_ref.shape[1]
    block = rows_ref[0]
    two = dot(stack_slots(block, 0, width), pair_ref[...], contract_rows)
    gate_ref[0] = two[:, :lanes]
    up_ref[0] = two[:, lanes:]
    down_ref[0] = dot(stack_slots(block, CAP, width), hidden_ref[...], contract_rows)


def outer(rows, pair, hidden):
    slices, sources, lanes = rows.shape
    width = lanes // (2 * CAP)
    units = hidden.shape[1]
    out = jax.ShapeDtypeStruct((1, slices * width, units), F32)
    flops = 2 * CAP * sources * slices * width * units * 3
    return pl.pallas_call(
        outer_kernel,
        grid=(slices,),
        out_shape=(out,) * 3,
        in_specs=[
            pl.BlockSpec((1, sources, lanes), lambda z: (z, 0, 0)),
            pl.BlockSpec(pair.shape, lambda z: (0, 0)),
            pl.BlockSpec(hidden.shape, lambda z: (0, 0)),
        ],
        out_specs=(pl.BlockSpec((1, width, units), lambda z: (0, z, 0)),) * 3,
        compiler_params=params(),
        cost_estimate=pl.CostEstimate(
            flops=flops, bytes_accessed=rows.size * 2 + 12 * slices * width * units, transcendentals=0
        ),
    )(rows, pair, hidden)


def total_kernel(parts_ref, out_ref):
    slices, rows, width = parts_ref.shape
    sources = rows // CAP
    total = parts_ref[0].astype(F32)
    for z in range(1, slices):
        total = total + parts_ref[z].astype(F32)
    total = total.astype(BF)
    for c in range(CAP):
        out_ref[:, c * width : (c + 1) * width] = total[c * sources : (c + 1) * sources, :]


def slice_total(parts):
    _, rows, width = parts.shape
    return pl.pallas_call(
        total_kernel,
        out_shape=jax.ShapeDtypeStruct((rows // CAP, CAP * width), BF),
        in_specs=vmem(1),
        out_specs=pl.BlockSpec(memory_space=pltpu.VMEM),
        compiler_params=params(),
    )(parts)


def combine_kernel(back_ref, pick_ref, out_ref):
    width = out_ref.shape[1]
    rows = stack_slots(back_ref[...], 0, width)
    out_ref[...] = dot(pick_ref[...], rows, contract_rows).astype(BF)


def combine(back, pick, shape):
    return pl.pallas_call(
        combine_kernel,
        out_shape=jax.ShapeDtypeStruct(shape, BF),
        in_specs=vmem(2),
        out_specs=pl.BlockSpec(memory_space=pltpu.VMEM),
        compiler_params=params(),
    )(back, pick)


def swap(x, axes):
    return lax.all_to_all(x, axes, split_axis=0, concat_axis=0, tiled=True)


def local(tokens, cotangent, routes, probs, matching, gate_weight, up_weight, down_weight):
    experts = matching.shape[0]
    model_width, units = gate_weight.shape[1:]
    piece = model_width // experts
    send, pick = pack(tokens, cotangent, routes, probs, matching)
    lanes = send.shape[1]
    first = jnp.concatenate(
        [w.reshape(experts, piece, units) for w in (gate_weight, up_weight, down_weight)]
        + [send.reshape(experts, lanes // units, units)],
        axis=1,
    )
    arrived = swap(first, "expert")
    rows = arrived[:, 3 * piece :, :].reshape(1, experts, lanes)
    rows = lax.all_gather(rows, "dp", axis=0, tiled=True)
    weights = swap(reorder(arrived, matching, 3 * piece), "expert")
    back, pair, hidden = expert(rows, weights)
    back = slice_total(swap(back, "dp"))
    back = swap(back.reshape(experts, 2, lanes // 4), "expert")
    gate_sum, up_sum, down_sum = outer(rows, pair, hidden)
    total = combine(back.reshape(experts, lanes // 2), pick, tokens.shape)
    return (total, gate_sum, up_sum, down_sum)


def solution(mesh):
    placed = (
        P("expert", "dp"),
        P("expert", "dp"),
        P("expert", None),
        P("expert", None),
        P(),
        P("expert", None, "dp"),
        P("expert", None, "dp"),
        P("expert", None, "dp"),
    )
    return jax.shard_map(
        local,
        mesh=mesh,
        in_specs=placed,
        out_specs=(
            P("expert", "dp"),
            P("expert", None, "dp"),
            P("expert", None, "dp"),
            P("expert", None, "dp"),
        ),
        check_vma=False,
    )
```

```python
import jax
import jax.numpy as jnp
from jax import lax
from jax.experimental import pallas as pl
from jax.experimental.pallas import tpu as pltpu
from jax.sharding import PartitionSpec as P

BF = jnp.bfloat16
F32 = jnp.float32
CAP = 5
MIB = 1024 * 1024

contract_rows = (((0,), (0,)), ((), ()))
contract_cols = (((1,), (1,)), ((), ()))


def params(whole=False):
    return pltpu.CompilerParams(vmem_limit_bytes=(63 if whole else 40) * MIB)


def vmem(n):
    return [pl.BlockSpec(memory_space=pltpu.VMEM)] * n


def dot(a, b, dims=(((1,), (0,)), ((), ()))):
    return lax.dot_general(a, b, dims, preferred_element_type=F32)


def pack_kernel(
    tok_hbm, cot_hbm, routes_hbm, probs_hbm, match_hbm,
    home_ref, away_ref, pick_ref,
    tok_ref, cot_ref, routes_ref, probs_ref, match_ref, sems,
):
    pairs = (
        (routes_hbm, routes_ref),
        (probs_hbm, probs_ref),
        (match_hbm, match_ref),
        (tok_hbm, tok_ref),
        (cot_hbm, cot_ref),
    )
    copies = [pltpu.make_async_copy(a, b, sems.at[i]) for i, (a, b) in enumerate(pairs)]
    for c in copies:
        c.start()
    for c in copies:
        c.wait()
    dests = match_ref.shape[1]
    rows = tok_ref.shape[0]
    width = tok_ref.shape[1]
    down = lax.broadcasted_iota(jnp.int32, (dests, dests), 0)
    across = lax.broadcasted_iota(jnp.int32, (dests, dests), 1)
    matched = jnp.sum(jnp.where(down == across, match_ref[...], 0), axis=1, keepdims=True)
    named = jnp.zeros((dests, rows), F32)
    weight = jnp.zeros((dests, rows), F32)
    experts = lax.broadcasted_iota(jnp.int32, (dests, rows), 0)
    for k in range(routes_ref.shape[0]):
        hit = experts == routes_ref[k : k + 1, :]
        named = named + jnp.where(hit, 1.0, 0.0)
        weight = weight + jnp.where(hit, probs_ref[k : k + 1, :], 0.0)
    before = lax.broadcasted_iota(jnp.int32, (rows, rows), 0) < lax.broadcasted_iota(
        jnp.int32, (rows, rows), 1
    )
    rank = dot(named.astype(BF), jnp.where(before, 1.0, 0.0).astype(BF))
    for c in range(CAP):
        pick = jnp.where((named > 0.5) & (jnp.abs(rank - c) < 0.5), 1.0, 0.0)
        scale = jnp.sum(pick * weight, axis=1, keepdims=True)
        pick = pick.astype(BF)
        pick_ref[c * dests : (c + 1) * dests, :] = pick
        home_ref[:, c * width : (c + 1) * width] = dot(pick, tok_ref[...]).astype(BF)
        grads = dot(pick, cot_ref[...]) * scale
        home_ref[:, (CAP + c) * width : (CAP + c + 1) * width] = grads.astype(BF)
    order = jnp.where(matched == across, 1.0, 0.0).astype(BF)
    away_ref[...] = dot(order, home_ref[...]).astype(BF)


def pack(tokens, cotangent, routes, probs, matching):
    dests = matching.shape[0]
    rows, width = tokens.shape
    buffer = jax.ShapeDtypeStruct((dests, 2 * CAP * width), BF)
    return pl.pallas_call(
        pack_kernel,
        out_shape=(buffer, buffer, jax.ShapeDtypeStruct((CAP * dests, rows), BF)),
        in_specs=[pl.BlockSpec(memory_space=pltpu.HBM)] * 5,
        out_specs=tuple(vmem(3)),
        scratch_shapes=[
            pltpu.VMEM(tokens.shape, BF),
            pltpu.VMEM(tokens.shape, BF),
            pltpu.VMEM(routes.shape[::-1], jnp.int32),
            pltpu.VMEM(routes.shape[::-1], F32),
            pltpu.VMEM((1, dests), jnp.int32),
            pltpu.SemaphoreType.DMA((5,)),
        ],
        compiler_params=params(whole=True),
    )(tokens, cotangent, routes.T, probs.T, matching.reshape(1, dests))


def stack_slots(block, first, width):
    return jnp.concatenate(
        [block[:, (first + c) * width : (first + c + 1) * width] for c in range(CAP)], axis=0
    )


def expert_kernel(rows_ref, gate_ref, up_ref, down_ref, send_ref):
    slices, sources, _ = rows_ref.shape
    width = rows_ref.shape[2] // (2 * CAP)
    lanes = gate_ref.shape[2]
    model = slices * width

    def both(z):
        part = slice(z * width, (z + 1) * width)
        return jnp.concatenate([gate_ref[0, part, :], up_ref[0, part, :]], axis=1)

    two = jnp.zeros((CAP * sources, 2 * lanes), F32)
    hidden_back = jnp.zeros((CAP * sources, lanes), F32)
    for z in range(slices):
        block = rows_ref[z]
        two = two + dot(stack_slots(block, 0, width), both(z))
        hidden_back = hidden_back + dot(
            stack_slots(block, CAP, width), down_ref[0, z * width : (z + 1) * width, :]
        )
    gate, upper = two[:, :lanes], two[:, lanes:]
    sig = jax.nn.sigmoid(gate)
    hidden = (gate * sig * upper).astype(BF)
    up_back = (hidden_back * gate * sig).astype(BF)
    gate_back = (hidden_back * upper * sig * (1.0 + gate * (1.0 - sig))).astype(BF)
    pair = jnp.concatenate([gate_back, up_back], axis=1)
    for z in range(slices):
        parts = dot(pair, both(z), contract_cols).astype(BF)
        for c in range(CAP):
            at = c * model + z * width
            send_ref[:, at : at + width] = parts[c * sources : (c + 1) * sources, :]
    for c in range(CAP):
        own = slice(c * sources, (c + 1) * sources)
        at = CAP * model + c * 3 * lanes
        send_ref[:, at : at + 2 * lanes] = pair[own, :]
        send_ref[:, at + 2 * lanes : at + 3 * lanes] = hidden[own, :]
    used = CAP * (model + 3 * lanes)
    send_ref[:, used:] = jnp.zeros((sources, send_ref.shape[1] - used), BF)


def expert(rows, w_gate, w_up, w_down):
    sources = rows.shape[1]
    model, units = w_gate.shape[1:]
    used = CAP * (model + 3 * units)
    return pl.pallas_call(
        expert_kernel,
        out_shape=jax.ShapeDtypeStruct((sources, -(-used // 1024) * 1024), BF),
        in_specs=vmem(4),
        out_specs=pl.BlockSpec(memory_space=pltpu.VMEM),
        compiler_params=params(),
    )(rows, w_gate, w_up, w_down)


def outer_kernel(rows_ref, factor_ref, gate_ref, up_ref, down_ref):
    width = rows_ref.shape[2] // (2 * CAP)
    lanes = gate_ref.shape[2]
    block = rows_ref[0]
    factors = stack_slots(factor_ref[...], 0, 3 * lanes)
    two = dot(stack_slots(block, 0, width), factors[:, : 2 * lanes], contract_rows)
    gate_ref[0] = two[:, :lanes]
    up_ref[0] = two[:, lanes:]
    down_ref[0] = dot(stack_slots(block, CAP, width), factors[:, 2 * lanes :], contract_rows)


def outer(rows, factors, units):
    slices, sources, lanes = rows.shape
    width = lanes // (2 * CAP)
    out = jax.ShapeDtypeStruct((1, slices * width, units), F32)
    flops = 2 * CAP * sources * slices * width * units * 3
    return pl.pallas_call(
        outer_kernel,
        grid=(slices,),
        out_shape=(out,) * 3,
        in_specs=[
            pl.BlockSpec((1, sources, lanes), lambda z: (z, 0, 0)),
            pl.BlockSpec(factors.shape, lambda z: (0, 0)),
        ],
        out_specs=(pl.BlockSpec((1, width, units), lambda z: (0, z, 0)),) * 3,
        compiler_params=params(whole=True),
        cost_estimate=pl.CostEstimate(
            flops=flops, bytes_accessed=rows.size * 2 + 12 * slices * width * units, transcendentals=0
        ),
    )(rows, factors)


def relay_kernel(back_ref, match_ref, out_ref):
    count = back_ref.shape[0]
    down = lax.broadcasted_iota(jnp.int32, (count, count), 0)
    across = lax.broadcasted_iota(jnp.int32, (count, count), 1)
    matched = jnp.sum(jnp.where(down == across, match_ref[...], 0), axis=1, keepdims=True)
    order = jnp.where(matched == across, 1.0, 0.0).astype(BF)
    out_ref[...] = dot(order, back_ref[:, back_ref.shape[1] - out_ref.shape[1] :]).astype(BF)


def relay(back, matching, lanes):
    count = back.shape[0]
    return pl.pallas_call(
        relay_kernel,
        out_shape=jax.ShapeDtypeStruct((count, lanes), BF),
        in_specs=vmem(2),
        out_specs=pl.BlockSpec(memory_space=pltpu.VMEM),
        compiler_params=params(),
    )(back, matching.reshape(1, count))


def combine_kernel(back_ref, pick_ref, out_ref):
    slices, _, width = out_ref.shape
    pick = pick_ref[...]
    for z in range(slices):
        rows = jnp.concatenate(
            [
                back_ref[:, (c * slices + z) * width : (c * slices + z + 1) * width]
                for c in range(CAP)
            ],
            axis=0,
        )
        out_ref[z] = dot(pick, rows, contract_rows).astype(BF)


def combine(back, pick, slices, width):
    rows = pick.shape[1]
    return pl.pallas_call(
        combine_kernel,
        out_shape=jax.ShapeDtypeStruct((slices, rows, width), BF),
        in_specs=vmem(2),
        out_specs=pl.BlockSpec(memory_space=pltpu.VMEM),
        compiler_params=params(),
        cost_estimate=pl.CostEstimate(
            flops=2 * pick.size * slices * width, bytes_accessed=2 * back.size, transcendentals=0
        ),
    )(back, pick)


def total_kernel(parts_ref, out_ref):
    total = parts_ref[0].astype(F32)
    for z in range(1, parts_ref.shape[0]):
        total = total + parts_ref[z].astype(F32)
    out_ref[...] = total.astype(BF)


def slice_total(parts):
    return pl.pallas_call(
        total_kernel,
        out_shape=jax.ShapeDtypeStruct(parts.shape[1:], BF),
        in_specs=vmem(1),
        out_specs=pl.BlockSpec(memory_space=pltpu.VMEM),
        compiler_params=params(),
    )(parts)


def swap(x, axes):
    return lax.all_to_all(x, axes, split_axis=0, concat_axis=0, tiled=True)


def spread(send):
    dests, lanes = send.shape
    rows = swap(send.reshape(dests, lanes // 128, 128), "expert").reshape(1, dests, lanes)
    return lax.all_gather(rows, "dp", axis=0, tiled=True)


def local(tokens, cotangent, routes, probs, matching, gate_weight, up_weight, down_weight):
    experts = matching.shape[0]
    model, units = gate_weight.shape[1:]
    width = tokens.shape[1]
    home, away, pick = pack(tokens, cotangent, routes, probs, matching)
    home_rows = spread(home)
    away_rows = spread(away)
    send = expert(home_rows, gate_weight, up_weight, down_weight)
    lanes = send.shape[1]
    back = swap(send.reshape(experts, lanes // 128, 128), "expert").reshape(experts, lanes)
    span = lanes - CAP * model
    moved = swap(relay(back, matching, span).reshape(experts, span // 128, 128), "expert")
    sums, moved = lax.optimization_barrier((combine(back, pick, model // width, width), moved))
    parts = swap(sums, "dp")
    gate_sum, up_sum, down_sum = outer(away_rows, moved.reshape(experts, span), units)
    return (slice_total(parts), gate_sum, up_sum, down_sum)


def solution(mesh):
    placed = (
        P("expert", "dp"),
        P("expert", "dp"),
        P("expert", None),
        P("expert", None),
        P(),
        P("expert", None, "dp"),
        P("expert", None, "dp"),
        P("expert", None, "dp"),
    )
    return jax.shard_map(
        local,
        mesh=mesh,
        in_specs=placed,
        out_specs=(
            P("expert", "dp"),
            P("expert", None, "dp"),
            P("expert", None, "dp"),
            P("expert", None, "dp"),
        ),
        check_vma=False,
    )
```

```python
import functools

import jax
import jax.numpy as jnp
from jax import lax
from jax.experimental import pallas as pl
from jax.experimental.pallas import tpu as pltpu
from jax.sharding import PartitionSpec as P

BF = jnp.bfloat16
F32 = jnp.float32
CAP = 5
MIB = 1024 * 1024
LANES = 128

contract_rows = (((0,), (0,)), ((), ()))
contract_cols = (((1,), (1,)), ((), ()))


def params(whole=False):
    return pltpu.CompilerParams(vmem_limit_bytes=(63 if whole else 40) * MIB)


def vmem(n):
    return [pl.BlockSpec(memory_space=pltpu.VMEM)] * n


def dot(a, b, dims=(((1,), (0,)), ((), ()))):
    return lax.dot_general(a, b, dims, preferred_element_type=F32)


def fold(block, scratch, out_ref):
    count, rows, _ = out_ref.shape
    for q in range(rows):
        scratch[pl.ds(q, count, stride=rows), :] = block(q)
    out_ref[...] = scratch[...].reshape(out_ref.shape).astype(BF)


def pack_kernel(
    tok_hbm, cot_hbm, routes_hbm, probs_hbm, match_hbm,
    home_ref, away_ref, pick_ref,
    tok_ref, cot_ref, routes_ref, probs_ref, match_ref, flat_ref, fold_ref, sems,
):
    pairs = (
        (routes_hbm, routes_ref),
        (probs_hbm, probs_ref),
        (match_hbm, match_ref),
        (tok_hbm, tok_ref),
        (cot_hbm, cot_ref),
    )
    copies = [pltpu.make_async_copy(a, b, sems.at[i]) for i, (a, b) in enumerate(pairs)]
    for c in copies:
        c.start()
    for c in copies:
        c.wait()
    dests = match_ref.shape[1]
    rows = tok_ref.shape[0]
    width = tok_ref.shape[1]
    down = lax.broadcasted_iota(jnp.int32, (dests, dests), 0)
    across = lax.broadcasted_iota(jnp.int32, (dests, dests), 1)
    matched = jnp.sum(jnp.where(down == across, match_ref[...], 0), axis=1, keepdims=True)
    named = jnp.zeros((dests, rows), F32)
    weight = jnp.zeros((dests, rows), F32)
    experts = lax.broadcasted_iota(jnp.int32, (dests, rows), 0)
    for k in range(routes_ref.shape[0]):
        hit = experts == routes_ref[k : k + 1, :]
        named = named + jnp.where(hit, 1.0, 0.0)
        weight = weight + jnp.where(hit, probs_ref[k : k + 1, :], 0.0)
    before = lax.broadcasted_iota(jnp.int32, (rows, rows), 0) < lax.broadcasted_iota(
        jnp.int32, (rows, rows), 1
    )
    rank = dot(named.astype(BF), jnp.where(before, 1.0, 0.0).astype(BF))
    for c in range(CAP):
        pick = jnp.where((named > 0.5) & (jnp.abs(rank - c) < 0.5), 1.0, 0.0)
        scale = jnp.sum(pick * weight, axis=1, keepdims=True)
        pick = pick.astype(BF)
        pick_ref[c * dests : (c + 1) * dests, :] = pick
        flat_ref[:, c * width : (c + 1) * width] = dot(pick, tok_ref[...])
        flat_ref[:, (CAP + c) * width : (CAP + c + 1) * width] = dot(pick, cot_ref[...]) * scale
    fold(lambda q: flat_ref[:, q * LANES : (q + 1) * LANES], fold_ref, home_ref)
    order = jnp.where(matched == across, 1.0, 0.0).astype(BF)
    flat_ref[...] = dot(order, flat_ref[...].astype(BF))
    fold(lambda q: flat_ref[:, q * LANES : (q + 1) * LANES], fold_ref, away_ref)


def pack(tokens, cotangent, routes, probs, matching):
    dests = matching.shape[0]
    rows, width = tokens.shape
    lanes = 2 * CAP * width
    buffer = jax.ShapeDtypeStruct((dests, lanes // LANES, LANES), BF)
    return pl.pallas_call(
        pack_kernel,
        out_shape=(buffer, buffer, jax.ShapeDtypeStruct((CAP * dests, rows), BF)),
        in_specs=[pl.BlockSpec(memory_space=pltpu.HBM)] * 5,
        out_specs=tuple(vmem(3)),
        scratch_shapes=[
            pltpu.VMEM(tokens.shape, BF),
            pltpu.VMEM(tokens.shape, BF),
            pltpu.VMEM(routes.shape[::-1], jnp.int32),
            pltpu.VMEM(routes.shape[::-1], F32),
            pltpu.VMEM((1, dests), jnp.int32),
            pltpu.VMEM((dests, lanes), F32),
            pltpu.VMEM((dests * lanes // LANES, LANES), F32),
            pltpu.SemaphoreType.DMA((5,)),
        ],
        compiler_params=params(whole=True),
    )(tokens, cotangent, routes.T, probs.T, matching.reshape(1, dests))


def stack_slots(block, first, width):
    return jnp.concatenate(
        [block[:, (first + c) * width : (first + c + 1) * width] for c in range(CAP)], axis=0
    )


def expert_kernel(rows_ref, gate_ref, up_ref, down_ref, parts_ref, factor_ref, fold_ref):
    slices, sources, _ = rows_ref.shape
    width = rows_ref.shape[2] // (2 * CAP)
    lanes = gate_ref.shape[2]

    def both(z):
        part = slice(z * width, (z + 1) * width)
        return jnp.concatenate([gate_ref[0, part, :], up_ref[0, part, :]], axis=1)

    two = jnp.zeros((CAP * sources, 2 * lanes), F32)
    hidden_back = jnp.zeros((CAP * sources, lanes), F32)
    for z in range(slices):
        block = rows_ref[z]
        two = two + dot(stack_slots(block, 0, width), both(z))
        hidden_back = hidden_back + dot(
            stack_slots(block, CAP, width), down_ref[0, z * width : (z + 1) * width, :]
        )
    gate, upper = two[:, :lanes], two[:, lanes:]
    sig = jax.nn.sigmoid(gate)
    hidden = (gate * sig * upper).astype(BF)
    up_back = (hidden_back * gate * sig).astype(BF)
    gate_back = (hidden_back * upper * sig * (1.0 + gate * (1.0 - sig))).astype(BF)
    pair = jnp.concatenate([gate_back, up_back], axis=1)
    for z in range(slices):
        parts_ref[z] = dot(pair, both(z), contract_cols).astype(BF)
    three = [v.astype(F32) for v in (gate_back, up_back, hidden)]
    blank = jnp.zeros((sources, LANES), F32)

    def block(q):
        c, k = divmod(q, 3)
        return three[k][c * sources : (c + 1) * sources, :] if c < CAP else blank

    fold(block, fold_ref, factor_ref)


def expert(rows, w_gate, w_up, w_down):
    slices, sources, lanes = rows.shape
    blocks = -(-CAP * 3 // 16) * 16
    return pl.pallas_call(
        expert_kernel,
        out_shape=(
            jax.ShapeDtypeStruct((slices, CAP * sources, lanes // (2 * CAP)), BF),
            jax.ShapeDtypeStruct((sources, blocks, LANES), BF),
        ),
        in_specs=vmem(4),
        out_specs=tuple(vmem(2)),
        scratch_shapes=[pltpu.VMEM((sources * blocks, LANES), F32)],
        compiler_params=params(),
    )(rows, w_gate, w_up, w_down)


def turn_kernel(offsets, me_ref, *refs):
    rows_hbm, (tokens_ref, grads_ref, rows_ref, sems) = refs[:-4], refs[-4:]
    width = rows_ref.shape[2] // (2 * CAP)
    copies = [
        pltpu.make_async_copy(r, rows_ref.at[i], sems.at[i]) for i, r in enumerate(rows_hbm)
    ]
    for c in copies:
        c.start()
    for i, c in enumerate(copies):
        c.wait()
        block = rows_ref[i]
        owner = lax.rem(me_ref[0] + (len(offsets) + offsets[i]), len(offsets))
        part = pl.ds(pl.multiple_of(owner * width, width), width)
        tokens_ref[part, :] = stack_slots(block, 0, width).T
        grads_ref[part, :] = stack_slots(block, CAP, width).T


def turn(me, offsets, rows):
    count = len(rows)
    sources, lanes = rows[0].shape
    out = jax.ShapeDtypeStruct((count * lanes // (2 * CAP), CAP * sources), BF)
    return pl.pallas_call(
        functools.partial(turn_kernel, offsets),
        out_shape=(out, out),
        in_specs=[pl.BlockSpec(memory_space=pltpu.SMEM)]
        + [pl.BlockSpec(memory_space=pltpu.HBM)] * count,
        out_specs=tuple(vmem(2)),
        scratch_shapes=[
            pltpu.VMEM((count, sources, lanes), BF),
            pltpu.SemaphoreType.DMA((count,)),
        ],
        compiler_params=params(),
        cost_estimate=pl.CostEstimate(
            flops=0, bytes_accessed=4 * count * sources * lanes, transcendentals=0
        ),
    )(me, *rows)


def outer_kernel(
    tokens_ref, grads_ref, moved_ref, gate_ref, up_ref, down_ref, wide_ref, factor_ref
):
    sources = moved_ref.shape[0]
    per = moved_ref.shape[1]
    lanes = gate_ref.shape[2]
    used = 3 * lanes // LANES

    @pl.when(pl.program_id(0) == 0)
    def _():
        wide_ref[...] = moved_ref[...].reshape(wide_ref.shape).astype(F32)
        for c in range(CAP):
            for k in range(used):
                block = wide_ref[pl.ds(c * used + k, sources, stride=per), :]
                factor_ref[c * sources : (c + 1) * sources, k * LANES : (k + 1) * LANES] = (
                    block.astype(BF)
                )

    two = dot(tokens_ref[...], factor_ref[:, : 2 * lanes])
    gate_ref[0] = two[:, :lanes]
    up_ref[0] = two[:, lanes:]
    down_ref[0] = dot(grads_ref[...], factor_ref[:, 2 * lanes :])


def outer(tokens, grads, moved, units):
    model, rows = tokens.shape
    steps = 4
    part = model // steps
    out = jax.ShapeDtypeStruct((1, model, units), F32)
    return pl.pallas_call(
        outer_kernel,
        grid=(steps,),
        out_shape=(out,) * 3,
        in_specs=[
            pl.BlockSpec((part, rows), lambda i: (i, 0)),
            pl.BlockSpec((part, rows), lambda i: (i, 0)),
            pl.BlockSpec(moved.shape, lambda i: (0, 0, 0)),
        ],
        out_specs=(pl.BlockSpec((1, part, units), lambda i: (0, i, 0)),) * 3,
        scratch_shapes=[
            pltpu.VMEM((moved.shape[0] * moved.shape[1], LANES), F32),
            pltpu.VMEM((rows, 3 * units), BF),
        ],
        compiler_params=params(),
        cost_estimate=pl.CostEstimate(
            flops=6 * rows * model * units,
            bytes_accessed=4 * tokens.size + 12 * model * units,
            transcendentals=0,
        ),
    )(tokens, grads, moved)


def relay_kernel(match_ref, src_ref, out_ref):
    for d in range(out_ref.shape[0]):
        out_ref[d] = src_ref[match_ref[d]]


def relay(blocks, matching):
    return pl.pallas_call(
        relay_kernel,
        out_shape=jax.ShapeDtypeStruct(blocks.shape, BF),
        in_specs=[pl.BlockSpec(memory_space=pltpu.SMEM)] + vmem(1),
        out_specs=pl.BlockSpec(memory_space=pltpu.VMEM),
        compiler_params=params(),
    )(matching, blocks)


def slots_kernel(rows_ref, out_ref):
    sources, width = out_ref.shape[0], rows_ref.shape[1]
    for c in range(CAP):
        out_ref[:, c * width : (c + 1) * width] = rows_ref[c * sources : (c + 1) * sources, :]


def slots_to_lanes(rows):
    count, width = rows.shape
    return pl.pallas_call(
        slots_kernel,
        out_shape=jax.ShapeDtypeStruct((count // CAP, CAP * width), BF),
        in_specs=vmem(1),
        out_specs=pl.BlockSpec(memory_space=pltpu.VMEM),
        compiler_params=params(),
    )(rows)


def combine_kernel(back_ref, pick_ref, out_ref):
    rows = stack_slots(back_ref[...], 0, out_ref.shape[1])
    out_ref[...] = dot(pick_ref[...], rows, contract_rows).astype(BF)


def combine(back, pick, shape):
    return pl.pallas_call(
        combine_kernel,
        out_shape=jax.ShapeDtypeStruct(shape, BF),
        in_specs=vmem(2),
        out_specs=pl.BlockSpec(memory_space=pltpu.VMEM),
        compiler_params=params(),
    )(back, pick)


def swap(x, axes):
    return lax.all_to_all(x, axes, split_axis=0, concat_axis=0, tiled=True)


def arrive(send):
    return swap(send, "expert").reshape(send.shape[0], send.shape[1] * LANES)


def around(x, step):
    count = lax.axis_size("dp")
    return lax.ppermute(x, "dp", [(i, (i + step) % count) for i in range(count)])


def collect(x):
    count = lax.axis_size("dp")
    found, offsets = [x], [0]
    right = left = x
    for k in range(1, count // 2 + 1):
        right = around(right, 1)
        found.append(right)
        offsets.append(-k)
        if k < count // 2:
            left = around(left, -1)
            found.append(left)
            offsets.append(k)
    return offsets, found


def local(tokens, cotangent, routes, probs, matching, gate_weight, up_weight, down_weight):
    experts = matching.shape[0]
    units = gate_weight.shape[2]
    width = tokens.shape[1]
    home, away, pick = pack(tokens, cotangent, routes, probs, matching)
    home_rows = lax.all_gather(arrive(home)[None], "dp", axis=0, tiled=True)
    home_rows, arrived = lax.optimization_barrier((home_rows, arrive(away)))
    offsets, away_rows = collect(arrived)
    parts, factors = expert(home_rows, gate_weight, up_weight, down_weight)
    pair_back = lax.psum_scatter(
        parts.reshape(-1, width), "dp", scatter_dimension=0, tiled=True
    )
    moved = swap(relay(swap(factors, "expert"), matching), "expert")
    pair_back, moved = lax.optimization_barrier((pair_back, moved))
    lanes = CAP * width
    back = swap(slots_to_lanes(pair_back).reshape(experts, 2, lanes // 2), "expert")
    turned, grads_turned = turn(lax.axis_index("dp").reshape(1), offsets, away_rows)
    gate_sum, up_sum, down_sum = outer(turned, grads_turned, moved, units)
    total = combine(back.reshape(experts, lanes), pick, tokens.shape)
    return (total, gate_sum, up_sum, down_sum)


def solution(mesh):
    placed = (
        P("expert", "dp"),
        P("expert", "dp"),
        P("expert", None),
        P("expert", None),
        P(),
        P("expert", None, "dp"),
        P("expert", None, "dp"),
        P("expert", None, "dp"),
    )
    return jax.shard_map(
        local,
        mesh=mesh,
        in_specs=placed,
        out_specs=(
            P("expert", "dp"),
            P("expert", None, "dp"),
            P("expert", None, "dp"),
            P("expert", None, "dp"),
        ),
        check_vma=False,
    )
```

```python
import functools

import jax
import jax.numpy as jnp
from jax import lax
from jax.experimental import pallas as pl
from jax.experimental.pallas import tpu as pltpu
from jax.sharding import PartitionSpec as P

BF = jnp.bfloat16
F32 = jnp.float32
CAP = 5
MIB = 1024 * 1024
LANES = 128

contract_rows = (((0,), (0,)), ((), ()))
contract_cols = (((1,), (1,)), ((), ()))


def params(whole=False):
    return pltpu.CompilerParams(vmem_limit_bytes=(63 if whole else 40) * MIB)


def vmem(n):
    return [pl.BlockSpec(memory_space=pltpu.VMEM)] * n


def dot(a, b, dims=(((1,), (0,)), ((), ()))):
    return lax.dot_general(a, b, dims, preferred_element_type=F32)


def fold(block, scratch, out_ref):
    count, rows, _ = out_ref.shape
    for q in range(rows):
        scratch[pl.ds(q, count, stride=rows), :] = block(q)
    out_ref[...] = scratch[: count * rows, :].reshape(out_ref.shape).astype(BF)


def pack_kernel(
    tok_hbm, cot_hbm, routes_hbm, probs_hbm, match_hbm,
    home_ref, away_ref, pick_ref,
    tok_ref, cot_ref, routes_ref, probs_ref, match_ref, flat_ref, fold_ref, sems,
):
    pairs = (
        (routes_hbm, routes_ref),
        (probs_hbm, probs_ref),
        (match_hbm, match_ref),
        (tok_hbm, tok_ref),
        (cot_hbm, cot_ref),
    )
    copies = [pltpu.make_async_copy(a, b, sems.at[i]) for i, (a, b) in enumerate(pairs)]
    for c in copies:
        c.start()
    for c in copies:
        c.wait()
    dests = match_ref.shape[1]
    rows = tok_ref.shape[0]
    width = tok_ref.shape[1]
    down = lax.broadcasted_iota(jnp.int32, (dests, dests), 0)
    across = lax.broadcasted_iota(jnp.int32, (dests, dests), 1)
    matched = jnp.sum(jnp.where(down == across, match_ref[...], 0), axis=1, keepdims=True)
    named = jnp.zeros((dests, rows), F32)
    weight = jnp.zeros((dests, rows), F32)
    experts = lax.broadcasted_iota(jnp.int32, (dests, rows), 0)
    for k in range(routes_ref.shape[0]):
        hit = experts == routes_ref[k : k + 1, :]
        named = named + jnp.where(hit, 1.0, 0.0)
        weight = weight + jnp.where(hit, probs_ref[k : k + 1, :], 0.0)
    before = lax.broadcasted_iota(jnp.int32, (rows, rows), 0) < lax.broadcasted_iota(
        jnp.int32, (rows, rows), 1
    )
    rank = dot(named.astype(BF), jnp.where(before, 1.0, 0.0).astype(BF))
    for c in range(CAP):
        pick = jnp.where((named > 0.5) & (jnp.abs(rank - c) < 0.5), 1.0, 0.0)
        scale = jnp.sum(pick * weight, axis=1, keepdims=True)
        pick = pick.astype(BF)
        pick_ref[c * dests : (c + 1) * dests, :] = pick
        flat_ref[:, c * width : (c + 1) * width] = dot(pick, tok_ref[...])
        flat_ref[:, (CAP + c) * width : (CAP + c + 1) * width] = dot(pick, cot_ref[...]) * scale
    fold(lambda q: flat_ref[:, q * LANES : (q + 1) * LANES], fold_ref, home_ref)
    order = jnp.where(matched == across, 1.0, 0.0).astype(BF)
    flat_ref[...] = dot(order, flat_ref[...].astype(BF))
    fold(lambda q: flat_ref[:, q * LANES : (q + 1) * LANES], fold_ref, away_ref)


def pack(tokens, cotangent, routes, probs, matching):
    dests = matching.shape[0]
    rows, width = tokens.shape
    lanes = 2 * CAP * width
    buffer = jax.ShapeDtypeStruct((dests, lanes // LANES, LANES), BF)
    return pl.pallas_call(
        pack_kernel,
        out_shape=(buffer, buffer, jax.ShapeDtypeStruct((CAP * dests, rows), BF)),
        in_specs=[pl.BlockSpec(memory_space=pltpu.HBM)] * 5,
        out_specs=tuple(vmem(3)),
        scratch_shapes=[
            pltpu.VMEM(tokens.shape, BF),
            pltpu.VMEM(tokens.shape, BF),
            pltpu.VMEM(routes.shape[::-1], jnp.int32),
            pltpu.VMEM(routes.shape[::-1], F32),
            pltpu.VMEM((1, dests), jnp.int32),
            pltpu.VMEM((dests, lanes), F32),
            pltpu.VMEM(((dests + 1) * lanes // LANES, LANES), F32),
            pltpu.SemaphoreType.DMA((5,)),
        ],
        compiler_params=params(whole=True),
    )(tokens, cotangent, routes.T, probs.T, matching.reshape(1, dests))


def stack_slots(block, first, width):
    return jnp.concatenate(
        [block[:, (first + c) * width : (first + c + 1) * width] for c in range(CAP)], axis=0
    )


def expert_kernel(rows_ref, gate_ref, up_ref, down_ref, parts_ref, factor_ref, fold_ref):
    slices, sources, _ = rows_ref.shape
    width = rows_ref.shape[2] // (2 * CAP)
    lanes = gate_ref.shape[2]

    def both(z):
        part = slice(z * width, (z + 1) * width)
        return jnp.concatenate([gate_ref[0, part, :], up_ref[0, part, :]], axis=1)

    two = jnp.zeros((CAP * sources, 2 * lanes), F32)
    hidden_back = jnp.zeros((CAP * sources, lanes), F32)
    for z in range(slices):
        block = rows_ref[z]
        two = two + dot(stack_slots(block, 0, width), both(z))
        hidden_back = hidden_back + dot(
            stack_slots(block, CAP, width), down_ref[0, z * width : (z + 1) * width, :]
        )
    gate, upper = two[:, :lanes], two[:, lanes:]
    sig = jax.nn.sigmoid(gate)
    hidden = (gate * sig * upper).astype(BF)
    up_back = (hidden_back * gate * sig).astype(BF)
    gate_back = (hidden_back * upper * sig * (1.0 + gate * (1.0 - sig))).astype(BF)
    pair = jnp.concatenate([gate_back, up_back], axis=1)
    for z in range(slices):
        parts_ref[z] = dot(pair, both(z), contract_cols).astype(BF)
    three = [v.astype(F32) for v in (gate_back, up_back, hidden)]
    blank = jnp.zeros((sources, LANES), F32)

    def block(q):
        c, k = divmod(q, 3)
        return three[k][c * sources : (c + 1) * sources, :] if c < CAP else blank

    fold(block, fold_ref, factor_ref)


def expert(rows, w_gate, w_up, w_down):
    slices, sources, lanes = rows.shape
    blocks = -(-CAP * 3 // 16) * 16
    return pl.pallas_call(
        expert_kernel,
        out_shape=(
            jax.ShapeDtypeStruct((slices, CAP * sources, lanes // (2 * CAP)), BF),
            jax.ShapeDtypeStruct((sources, blocks, LANES), BF),
        ),
        in_specs=vmem(4),
        out_specs=tuple(vmem(2)),
        scratch_shapes=[pltpu.VMEM(((sources + 1) * blocks, LANES), F32)],
        compiler_params=params(),
    )(rows, w_gate, w_up, w_down)


def turn_kernel(offsets, me_ref, *refs):
    rows_hbm, (tokens_ref, grads_ref, rows_ref, sems) = refs[:-4], refs[-4:]
    width = rows_ref.shape[2] // (2 * CAP)
    copies = [
        pltpu.make_async_copy(r, rows_ref.at[i], sems.at[i]) for i, r in enumerate(rows_hbm)
    ]
    for c in copies:
        c.start()
    for i, c in enumerate(copies):
        c.wait()
        block = rows_ref[i]
        owner = lax.rem(me_ref[0] + (len(offsets) + offsets[i]), len(offsets))
        part = pl.ds(pl.multiple_of(owner * width, width), width)
        tokens_ref[part, :] = stack_slots(block, 0, width).T
        grads_ref[part, :] = stack_slots(block, CAP, width).T


def turn(me, offsets, rows):
    count = len(rows)
    sources, lanes = rows[0].shape
    out = jax.ShapeDtypeStruct((count * lanes // (2 * CAP), CAP * sources), BF)
    return pl.pallas_call(
        functools.partial(turn_kernel, offsets),
        out_shape=(out, out),
        in_specs=[pl.BlockSpec(memory_space=pltpu.SMEM)]
        + [pl.BlockSpec(memory_space=pltpu.HBM)] * count,
        out_specs=tuple(vmem(2)),
        scratch_shapes=[
            pltpu.VMEM((count, sources, lanes), BF),
            pltpu.SemaphoreType.DMA((count,)),
        ],
        compiler_params=params(),
        cost_estimate=pl.CostEstimate(
            flops=0, bytes_accessed=4 * count * sources * lanes, transcendentals=0
        ),
    )(me, *rows)


def outer_kernel(
    tokens_ref, grads_ref, moved_ref, gate_ref, up_ref, down_ref, wide_ref, factor_ref
):
    sources = moved_ref.shape[0]
    per = moved_ref.shape[1]
    lanes = gate_ref.shape[2]
    used = 3 * lanes // LANES

    @pl.when(pl.program_id(0) == 0)
    def _():
        wide_ref[: sources * per, :] = moved_ref[...].reshape(sources * per, LANES).astype(F32)
        for c in range(CAP):
            for k in range(used):
                block = wide_ref[pl.ds(c * used + k, sources, stride=per), :]
                factor_ref[c * sources : (c + 1) * sources, k * LANES : (k + 1) * LANES] = (
                    block.astype(BF)
                )

    two = dot(tokens_ref[...], factor_ref[:, : 2 * lanes])
    gate_ref[0] = two[:, :lanes]
    up_ref[0] = two[:, lanes:]
    down_ref[0] = dot(grads_ref[...], factor_ref[:, 2 * lanes :])


def outer(tokens, grads, moved, units):
    model, rows = tokens.shape
    steps = 4
    part = model // steps
    out = jax.ShapeDtypeStruct((1, model, units), F32)
    return pl.pallas_call(
        outer_kernel,
        grid=(steps,),
        out_shape=(out,) * 3,
        in_specs=[
            pl.BlockSpec((part, rows), lambda i: (i, 0)),
            pl.BlockSpec((part, rows), lambda i: (i, 0)),
            pl.BlockSpec(moved.shape, lambda i: (0, 0, 0)),
        ],
        out_specs=(pl.BlockSpec((1, part, units), lambda i: (0, i, 0)),) * 3,
        scratch_shapes=[
            pltpu.VMEM(((moved.shape[0] + 1) * moved.shape[1], LANES), F32),
            pltpu.VMEM((rows, 3 * units), BF),
        ],
        compiler_params=params(),
        cost_estimate=pl.CostEstimate(
            flops=6 * rows * model * units,
            bytes_accessed=4 * tokens.size + 12 * model * units,
            transcendentals=0,
        ),
    )(tokens, grads, moved)


def relay_kernel(match_ref, src_ref, out_ref):
    for d in range(out_ref.shape[0]):
        out_ref[d] = src_ref[match_ref[d]]


def relay(blocks, matching):
    return pl.pallas_call(
        relay_kernel,
        out_shape=jax.ShapeDtypeStruct(blocks.shape, BF),
        in_specs=[pl.BlockSpec(memory_space=pltpu.SMEM)] + vmem(1),
        out_specs=pl.BlockSpec(memory_space=pltpu.VMEM),
        compiler_params=params(),
    )(matching, blocks)


def slots_kernel(rows_ref, out_ref):
    sources, width = out_ref.shape[0], rows_ref.shape[1]
    for c in range(CAP):
        out_ref[:, c * width : (c + 1) * width] = rows_ref[c * sources : (c + 1) * sources, :]


def slots_to_lanes(rows):
    count, width = rows.shape
    return pl.pallas_call(
        slots_kernel,
        out_shape=jax.ShapeDtypeStruct((count // CAP, CAP * width), BF),
        in_specs=vmem(1),
        out_specs=pl.BlockSpec(memory_space=pltpu.VMEM),
        compiler_params=params(),
    )(rows)


def combine_kernel(back_ref, pick_ref, out_ref):
    rows = stack_slots(back_ref[...], 0, out_ref.shape[1])
    out_ref[...] = dot(pick_ref[...], rows, contract_rows).astype(BF)


def combine(back, pick, shape):
    return pl.pallas_call(
        combine_kernel,
        out_shape=jax.ShapeDtypeStruct(shape, BF),
        in_specs=vmem(2),
        out_specs=pl.BlockSpec(memory_space=pltpu.VMEM),
        compiler_params=params(),
    )(back, pick)


def swap(x, axes):
    return lax.all_to_all(x, axes, split_axis=0, concat_axis=0, tiled=True)


def arrive(send):
    return swap(send, "expert").reshape(send.shape[0], send.shape[1] * LANES)


def around(x, step):
    count = lax.axis_size("dp")
    return lax.ppermute(x, "dp", [(i, (i + step) % count) for i in range(count)])


def collect(x):
    count = lax.axis_size("dp")
    found, offsets = [x], [0]
    right = left = x
    for k in range(1, count // 2 + 1):
        right = around(right, 1)
        found.append(right)
        offsets.append(-k)
        if k < count // 2:
            left = around(left, -1)
            found.append(left)
            offsets.append(k)
    return offsets, found


def local(tokens, cotangent, routes, probs, matching, gate_weight, up_weight, down_weight):
    experts = matching.shape[0]
    units = gate_weight.shape[2]
    width = tokens.shape[1]
    home, away, pick = pack(tokens, cotangent, routes, probs, matching)
    home_rows = lax.all_gather(arrive(home)[None], "dp", axis=0, tiled=True)
    home_rows, arrived = lax.optimization_barrier((home_rows, arrive(away)))
    offsets, away_rows = collect(arrived)
    parts, factors = expert(home_rows, gate_weight, up_weight, down_weight)
    pair_back = lax.psum_scatter(
        parts.reshape(-1, width), "dp", scatter_dimension=0, tiled=True
    )
    moved = swap(relay(swap(factors, "expert"), matching), "expert")
    pair_back, moved = lax.optimization_barrier((pair_back, moved))
    lanes = CAP * width
    back = swap(slots_to_lanes(pair_back).reshape(experts, 2, lanes // 2), "expert")
    turned, grads_turned = turn(lax.axis_index("dp").reshape(1), offsets, away_rows)
    gate_sum, up_sum, down_sum = outer(turned, grads_turned, moved, units)
    total = combine(back.reshape(experts, lanes), pick, tokens.shape)
    return (total, gate_sum, up_sum, down_sum)


def solution(mesh):
    placed = (
        P("expert", "dp"),
        P("expert", "dp"),
        P("expert", None),
        P("expert", None),
        P(),
        P("expert", None, "dp"),
        P("expert", None, "dp"),
        P("expert", None, "dp"),
    )
    return jax.shard_map(
        local,
        mesh=mesh,
        in_specs=placed,
        out_specs=(
            P("expert", "dp"),
            P("expert", None, "dp"),
            P("expert", None, "dp"),
            P("expert", None, "dp"),
        ),
        check_vma=False,
    )
```

```python
import functools

import jax
import jax.numpy as jnp
from jax import lax
from jax.experimental import pallas as pl
from jax.experimental.pallas import tpu as pltpu
from jax.sharding import PartitionSpec as P

BF = jnp.bfloat16
F32 = jnp.float32
CAP = 5
MIB = 1024 * 1024
LANES = 128

contract_rows = (((0,), (0,)), ((), ()))
contract_cols = (((1,), (1,)), ((), ()))


def params(whole=False):
    return pltpu.CompilerParams(vmem_limit_bytes=(63 if whole else 40) * MIB)


def vmem(n):
    return [pl.BlockSpec(memory_space=pltpu.VMEM)] * n


def dot(a, b, dims=(((1,), (0,)), ((), ()))):
    return lax.dot_general(a, b, dims, preferred_element_type=F32)


def fold(block, scratch, out_ref):
    count, rows, _ = out_ref.shape
    for q in range(rows):
        scratch[pl.ds(q, count, stride=rows), :] = block(q)
    out_ref[...] = scratch[: count * rows, :].reshape(out_ref.shape).astype(BF)


def pack_kernel(
    tok_hbm, cot_hbm, routes_hbm, probs_hbm, match_hbm,
    home_ref, away_ref, pick_ref,
    tok_ref, cot_ref, routes_ref, probs_ref, match_ref, flat_ref, fold_ref, sems,
):
    pairs = (
        (routes_hbm, routes_ref),
        (probs_hbm, probs_ref),
        (match_hbm, match_ref),
        (tok_hbm, tok_ref),
        (cot_hbm, cot_ref),
    )
    copies = [pltpu.make_async_copy(a, b, sems.at[i]) for i, (a, b) in enumerate(pairs)]
    for c in copies:
        c.start()
    for c in copies:
        c.wait()
    dests = match_ref.shape[1]
    rows = tok_ref.shape[0]
    width = tok_ref.shape[1]
    down = lax.broadcasted_iota(jnp.int32, (dests, dests), 0)
    across = lax.broadcasted_iota(jnp.int32, (dests, dests), 1)
    matched = jnp.sum(jnp.where(down == across, match_ref[...], 0), axis=1, keepdims=True)
    named = jnp.zeros((dests, rows), F32)
    weight = jnp.zeros((dests, rows), F32)
    experts = lax.broadcasted_iota(jnp.int32, (dests, rows), 0)
    for k in range(routes_ref.shape[0]):
        hit = experts == routes_ref[k : k + 1, :]
        named = named + jnp.where(hit, 1.0, 0.0)
        weight = weight + jnp.where(hit, probs_ref[k : k + 1, :], 0.0)
    before = lax.broadcasted_iota(jnp.int32, (rows, rows), 0) < lax.broadcasted_iota(
        jnp.int32, (rows, rows), 1
    )
    rank = dot(named.astype(BF), jnp.where(before, 1.0, 0.0).astype(BF))
    for c in range(CAP):
        pick = jnp.where((named > 0.5) & (jnp.abs(rank - c) < 0.5), 1.0, 0.0)
        scale = jnp.sum(pick * weight, axis=1, keepdims=True)
        pick = pick.astype(BF)
        pick_ref[c * dests : (c + 1) * dests, :] = pick
        flat_ref[:, c * width : (c + 1) * width] = dot(pick, tok_ref[...])
        flat_ref[:, (CAP + c) * width : (CAP + c + 1) * width] = dot(pick, cot_ref[...]) * scale
    fold(lambda q: flat_ref[:, q * LANES : (q + 1) * LANES], fold_ref, home_ref)
    order = jnp.where(matched == across, 1.0, 0.0).astype(BF)
    flat_ref[...] = dot(order, flat_ref[...].astype(BF))
    fold(lambda q: flat_ref[:, q * LANES : (q + 1) * LANES], fold_ref, away_ref)


def pack(tokens, cotangent, routes, probs, matching):
    dests = matching.shape[0]
    rows, width = tokens.shape
    lanes = 2 * CAP * width
    buffer = jax.ShapeDtypeStruct((dests, lanes // LANES, LANES), BF)
    return pl.pallas_call(
        pack_kernel,
        out_shape=(buffer, buffer, jax.ShapeDtypeStruct((CAP * dests, rows), BF)),
        in_specs=[pl.BlockSpec(memory_space=pltpu.HBM)] * 5,
        out_specs=tuple(vmem(3)),
        scratch_shapes=[
            pltpu.VMEM(tokens.shape, BF),
            pltpu.VMEM(tokens.shape, BF),
            pltpu.VMEM(routes.shape[::-1], jnp.int32),
            pltpu.VMEM(routes.shape[::-1], F32),
            pltpu.VMEM((1, dests), jnp.int32),
            pltpu.VMEM((dests, lanes), F32),
            pltpu.VMEM(((dests + 1) * lanes // LANES, LANES), F32),
            pltpu.SemaphoreType.DMA((5,)),
        ],
        compiler_params=params(whole=True),
    )(tokens, cotangent, routes.T, probs.T, matching.reshape(1, dests))


def stack_slots(block, first, width):
    return jnp.concatenate(
        [block[:, (first + c) * width : (first + c + 1) * width] for c in range(CAP)], axis=0
    )


def expert_kernel(rows_ref, gate_ref, up_ref, down_ref, parts_ref, factor_ref, fold_ref):
    slices, sources, _ = rows_ref.shape
    width = rows_ref.shape[2] // (2 * CAP)
    lanes = gate_ref.shape[2]

    def both(z):
        part = slice(z * width, (z + 1) * width)
        return jnp.concatenate([gate_ref[0, part, :], up_ref[0, part, :]], axis=1)

    two = jnp.zeros((CAP * sources, 2 * lanes), F32)
    hidden_back = jnp.zeros((CAP * sources, lanes), F32)
    for z in range(slices):
        block = rows_ref[z]
        two = two + dot(stack_slots(block, 0, width), both(z))
        hidden_back = hidden_back + dot(
            stack_slots(block, CAP, width), down_ref[0, z * width : (z + 1) * width, :]
        )
    gate, upper = two[:, :lanes], two[:, lanes:]
    sig = jax.nn.sigmoid(gate)
    hidden = (gate * sig * upper).astype(BF)
    up_back = (hidden_back * gate * sig).astype(BF)
    gate_back = (hidden_back * upper * sig * (1.0 + gate * (1.0 - sig))).astype(BF)
    pair = jnp.concatenate([gate_back, up_back], axis=1)
    for z in range(slices):
        parts_ref[z] = dot(pair, both(z), contract_cols).astype(BF)
    three = [v.astype(F32) for v in (gate_back, up_back, hidden)]
    blank = jnp.zeros((sources, LANES), F32)

    def block(q):
        c, k = divmod(q, 3)
        return three[k][c * sources : (c + 1) * sources, :] if c < CAP else blank

    fold(block, fold_ref, factor_ref)


def expert(rows, w_gate, w_up, w_down):
    slices, sources, lanes = rows.shape
    blocks = -(-CAP * 3 // 16) * 16
    return pl.pallas_call(
        expert_kernel,
        out_shape=(
            jax.ShapeDtypeStruct((slices, CAP * sources, lanes // (2 * CAP)), BF),
            jax.ShapeDtypeStruct((sources, blocks, LANES), BF),
        ),
        in_specs=vmem(4),
        out_specs=tuple(vmem(2)),
        scratch_shapes=[pltpu.VMEM(((sources + 1) * blocks, LANES), F32)],
        compiler_params=params(),
    )(rows, w_gate, w_up, w_down)


def turn_kernel(offsets, me_ref, *refs):
    rows_hbm, (tokens_ref, grads_ref, rows_ref, sems) = refs[:-4], refs[-4:]
    width = rows_ref.shape[2] // (2 * CAP)
    copies = [
        pltpu.make_async_copy(r, rows_ref.at[i], sems.at[i]) for i, r in enumerate(rows_hbm)
    ]
    for c in copies:
        c.start()
    for i, c in enumerate(copies):
        c.wait()
        block = rows_ref[i]
        owner = lax.rem(me_ref[0] + (len(offsets) + offsets[i]), len(offsets))
        part = pl.ds(pl.multiple_of(owner * width, width), width)
        tokens_ref[part, :] = stack_slots(block, 0, width).T
        grads_ref[part, :] = stack_slots(block, CAP, width).T


def turn(me, offsets, rows):
    count = len(rows)
    sources, lanes = rows[0].shape
    out = jax.ShapeDtypeStruct((count * lanes // (2 * CAP), CAP * sources), BF)
    return pl.pallas_call(
        functools.partial(turn_kernel, offsets),
        out_shape=(out, out),
        in_specs=[pl.BlockSpec(memory_space=pltpu.SMEM)]
        + [pl.BlockSpec(memory_space=pltpu.HBM)] * count,
        out_specs=tuple(vmem(2)),
        scratch_shapes=[
            pltpu.VMEM((count, sources, lanes), BF),
            pltpu.SemaphoreType.DMA((count,)),
        ],
        compiler_params=params(),
        cost_estimate=pl.CostEstimate(
            flops=0, bytes_accessed=4 * count * sources * lanes, transcendentals=0
        ),
    )(me, *rows)


def outer_kernel(
    tokens_ref, grads_ref, moved_ref, gate_ref, up_ref, down_ref, wide_ref, factor_ref
):
    sources = moved_ref.shape[0]
    per = moved_ref.shape[1]
    lanes = gate_ref.shape[2]
    used = 3 * lanes // LANES

    @pl.when(pl.program_id(0) == 0)
    def _():
        wide_ref[: sources * per, :] = moved_ref[...].reshape(sources * per, LANES).astype(F32)
        for c in range(CAP):
            for k in range(used):
                block = wide_ref[pl.ds(c * used + k, sources, stride=per), :]
                factor_ref[c * sources : (c + 1) * sources, k * LANES : (k + 1) * LANES] = (
                    block.astype(BF)
                )

    two = dot(tokens_ref[...], factor_ref[:, : 2 * lanes])
    gate_ref[0] = two[:, :lanes]
    up_ref[0] = two[:, lanes:]
    down_ref[0] = dot(grads_ref[...], factor_ref[:, 2 * lanes :])


def outer(tokens, grads, moved, units):
    model, rows = tokens.shape
    steps = 4
    part = model // steps
    out = jax.ShapeDtypeStruct((1, model, units), F32)
    return pl.pallas_call(
        outer_kernel,
        grid=(steps,),
        out_shape=(out,) * 3,
        in_specs=[
            pl.BlockSpec((part, rows), lambda i: (i, 0)),
            pl.BlockSpec((part, rows), lambda i: (i, 0)),
            pl.BlockSpec(moved.shape, lambda i: (0, 0, 0)),
        ],
        out_specs=(pl.BlockSpec((1, part, units), lambda i: (0, i, 0)),) * 3,
        scratch_shapes=[
            pltpu.VMEM(((moved.shape[0] + 1) * moved.shape[1], LANES), F32),
            pltpu.VMEM((rows, 3 * units), BF),
        ],
        compiler_params=params(),
        cost_estimate=pl.CostEstimate(
            flops=6 * rows * model * units,
            bytes_accessed=4 * tokens.size + 12 * model * units,
            transcendentals=0,
        ),
    )(tokens, grads, moved)


def relay_kernel(match_ref, src_ref, out_ref):
    for d in range(out_ref.shape[0]):
        out_ref[d] = src_ref[match_ref[d]]


def relay(blocks, matching):
    return pl.pallas_call(
        relay_kernel,
        out_shape=jax.ShapeDtypeStruct(blocks.shape, BF),
        in_specs=[pl.BlockSpec(memory_space=pltpu.SMEM)] + vmem(1),
        out_specs=pl.BlockSpec(memory_space=pltpu.VMEM),
        compiler_params=params(),
    )(matching, blocks)


def combine_kernel(back_ref, pick_ref, out_ref):
    rows = stack_slots(back_ref[...], 0, out_ref.shape[1])
    out_ref[...] = dot(pick_ref[...], rows, contract_rows).astype(BF)


def combine(back, pick, shape):
    return pl.pallas_call(
        combine_kernel,
        out_shape=jax.ShapeDtypeStruct(shape, BF),
        in_specs=vmem(2),
        out_specs=pl.BlockSpec(memory_space=pltpu.VMEM),
        compiler_params=params(),
    )(back, pick)


def swap(x, axes):
    return lax.all_to_all(x, axes, split_axis=0, concat_axis=0, tiled=True)


def arrive(send):
    return swap(send, "expert").reshape(send.shape[0], send.shape[1] * LANES)


def around(x, step):
    count = lax.axis_size("dp")
    return lax.ppermute(x, "dp", [(i, (i + step) % count) for i in range(count)])


def collect(x):
    count = lax.axis_size("dp")
    found, offsets = [x], [0]
    right = left = x
    for k in range(1, count // 2 + 1):
        right = around(right, 1)
        found.append(right)
        offsets.append(-k)
        if k < count // 2:
            left = around(left, -1)
            found.append(left)
            offsets.append(k)
    return offsets, found


def local(tokens, cotangent, routes, probs, matching, gate_weight, up_weight, down_weight):
    experts = matching.shape[0]
    units = gate_weight.shape[2]
    width = tokens.shape[1]
    home, away, pick = pack(tokens, cotangent, routes, probs, matching)
    home_rows = lax.all_gather(arrive(home)[None], "dp", axis=0, tiled=True)
    home_rows, arrived = lax.optimization_barrier((home_rows, arrive(away)))
    offsets, away_rows = collect(arrived)
    parts, factors = expert(home_rows, gate_weight, up_weight, down_weight)
    pair_back = lax.psum_scatter(
        parts.reshape(-1, width), "dp", scatter_dimension=0, tiled=True
    )
    moved = swap(relay(swap(factors, "expert"), matching), "expert")
    pair_back, moved = lax.optimization_barrier((pair_back, moved))
    lanes = CAP * width
    back = pair_back.reshape(CAP, experts, width).transpose(1, 0, 2)
    back = swap(back.reshape(experts, 2, lanes // 2), "expert")
    turned, grads_turned = turn(lax.axis_index("dp").reshape(1), offsets, away_rows)
    gate_sum, up_sum, down_sum = outer(turned, grads_turned, moved, units)
    total = combine(back.reshape(experts, lanes), pick, tokens.shape)
    return (total, gate_sum, up_sum, down_sum)


def solution(mesh):
    placed = (
        P("expert", "dp"),
        P("expert", "dp"),
        P("expert", None),
        P("expert", None),
        P(),
        P("expert", None, "dp"),
        P("expert", None, "dp"),
        P("expert", None, "dp"),
    )
    return jax.shard_map(
        local,
        mesh=mesh,
        in_specs=placed,
        out_specs=(
            P("expert", "dp"),
            P("expert", None, "dp"),
            P("expert", None, "dp"),
            P("expert", None, "dp"),
        ),
        check_vma=False,
    )
```
